32 devices in a mesh: dp: 8 (over y, x, core), tensor: 4 (over z).
Axes of the slice: x: 2, y: 2, z: 4, core: 2. Of those that a mesh axis runs over, the one named last changes fastest.
Arguments:
- hidden: bfloat16 [1024, 16384], P('dp'), may hold values from -6 to 6
- context: bfloat16 [1024, 16384], P('dp', 'tensor'), may hold values from -6 to 6
- query_weight: bfloat16 [16384, 16384], P(('dp', 'tensor')), may hold values from -0.046875 to 0.046875
- key_projection_rows: bfloat16 [16384, 1024], P(('dp', 'tensor')), may hold values from -0.046875 to 0.046875
- value_weight: bfloat16 [16384, 1024], P(('dp', 'tensor')), may hold values from -0.046875 to 0.046875
- query_lower_factor: bfloat16 [16384, 64], P(('dp', 'tensor')), may hold values from -0.75 to 0.75
- key_down: bfloat16 [16384, 64], P(('dp', 'tensor')), may hold values from -0.75 to 0.75
- value_down: bfloat16 [16384, 64], P(('dp', 'tensor')), may hold values from -0.75 to 0.75
- query_up: bfloat16 [64, 16384], P(None, ('dp', 'tensor')), may hold values from -0.01171875 to 0.01171875
- key_up: bfloat16 [64, 1024], replicated, may hold values from -0.01171875 to 0.01171875
- value_up: bfloat16 [64, 1024], replicated, may hold values from -0.01171875 to 0.01171875
- output_weight: bfloat16 [16384, 16384], P(('dp', 'tensor')), may hold values from -0.046875 to 0.046875
- output_down: bfloat16 [16384, 64], P(('dp', 'tensor')), may hold values from -0.75 to 0.75
- output_up: bfloat16 [64, 16384], P(None, ('dp', 'tensor')), may hold values from -0.01171875 to 0.01171875
- slice_group: int32 [8], replicated, may hold values from 0 to 7, each once
Outputs:
- merged_qkv: bfloat16 [16384, 18432], P('dp', 'tensor')
- merged_output: bfloat16 [16384, 16384], P('tensor', 'dp')
- projections: bfloat16 [1024, 18432], P('dp', 'tensor')
- attention_output: bfloat16 [1024, 16384], P('tensor', 'dp')
The draws below stay inside these ranges and needn't reach their ends.
Inputs may be any that keep to these rules, and one draw needn't show every extreme that they name: Serving slice t holds the key-value groups slice_group[t*2] .. slice_group[t*2 + 1]; every group appears once.
All inputs are finite; a program needn't handle non-finite values.
Results may differ from the reference program's by a relative error of at most 0.012.
Values may be sent and summed in bfloat16 or wider, within the bound.
No kernel may reach another device: no remote copies, remote signals or barrier semaphores. Data moves between devices by JAX's collectives and lax.ppermute only.
A program may use at most 320 MiB of HBM per device.

```python
import jax
import jax.numpy as jnp
from jax import lax

D = 16384
KVH = 8
HD = 128
RANK = 64
TOKENS = 1024
QD = 16384
KVD = 1024
GQ = 2048
N_DP = 8
N_TENSOR = 4


def steps_of(key, extent, split, least, largest):
    level = 1.0
    for dim, blocks in split:
        heights = jax.random.uniform(jax.random.fold_in(jax.random.fold_in(key, 6), dim), (blocks,), jnp.float32, least / len(split), largest / len(split))
        level = level * jnp.repeat(jnp.exp(heights), extent[dim] // blocks).reshape((-1,) + (1,) * (len(extent) - 1 - dim))
    return level


def noise(rng, shape, deviation, limit, split=(), kind=jnp.bfloat16):
    level = steps_of(rng, shape, split, -0.22, 0.18) if split else 1.0
    drawn = jax.random.normal(rng, shape, jnp.float32) * deviation * level
    return jnp.minimum(jnp.maximum(drawn, -limit), limit).astype(kind)


def setup_inputs(seed: int = 0) -> dict:
    keys = jax.random.split(jax.random.key(seed), 16)
    return {
        "hidden": noise(keys[0], (TOKENS, D), 1.0, 6.0, ((0, 8),)),
        "context": noise(keys[1], (TOKENS, QD), 1.0, 6.0, ((0, 8), (1, 4))),
        "query_weight": noise(keys[2], (D, QD), D ** -0.5, 0.046875, ((0, 32),)),
        "key_projection_rows": noise(keys[3], (D, KVD), D ** -0.5, 0.046875, ((0, 32),)),
        "value_weight": noise(keys[4], (D, KVD), D ** -0.5, 0.046875, ((0, 32),)),
        "query_lower_factor": noise(keys[5], (D, RANK), RANK ** -0.5, 0.75, ((0, 32),)),
        "key_down": noise(keys[6], (D, RANK), RANK ** -0.5, 0.75, ((0, 32),)),
        "value_down": noise(keys[7], (D, RANK), RANK ** -0.5, 0.75, ((0, 32),)),
        "query_up": noise(keys[8], (RANK, QD), (16 * D) ** -0.5, 0.01171875, ((1, 32),)),
        "key_up": noise(keys[9], (RANK, KVD), (16 * D) ** -0.5, 0.01171875),
        "value_up": noise(keys[10], (RANK, KVD), (16 * D) ** -0.5, 0.01171875),
        "output_weight": noise(keys[11], (QD, D), QD ** -0.5, 0.046875, ((0, 32),)),
        "output_down": noise(keys[12], (QD, RANK), RANK ** -0.5, 0.75, ((0, 32),)),
        "output_up": noise(keys[13], (RANK, D), (16 * QD) ** -0.5, 0.01171875, ((1, 32),)),
        "slice_group": jax.random.permutation(keys[14], KVH).astype(jnp.int32),
    }


adapter_scale_factor = 2.0


def merge_adapter(frozen_base_matrix, down_factor, up_factor):
    adapter_update = jnp.dot(down_factor, up_factor, preferred_element_type=jnp.float32)
    return (frozen_base_matrix.astype(jnp.float32) + adapter_scale_factor * adapter_update).astype(jnp.bfloat16)


def per_block_total(left, right, pieces):
    width = left.shape[1] // pieces

    def add_block(total, index):
        left_block = lax.dynamic_slice_in_dim(left, index * width, width, 1)
        right_block = lax.dynamic_slice_in_dim(right, index * width, width, 0)
        term = jnp.dot(left_block, right_block, preferred_element_type=jnp.float32)
        rounded = lax.optimization_barrier(term.astype(jnp.bfloat16)).astype(jnp.float32)
        return total + rounded, None

    start_total = jnp.zeros((left.shape[0], right.shape[1]), jnp.float32)
    total = lax.scan(add_block, start_total, jnp.arange(pieces, dtype=jnp.int32))[0]
    return total.astype(jnp.bfloat16)


def reference(hidden, context, query_weight, key_projection_rows, value_weight, query_lower_factor, key_down, value_down,
              query_up, key_up, value_up, output_weight, output_down, output_up, slice_group):
    merged_query = merge_adapter(query_weight, query_lower_factor, query_up)
    merged_key = merge_adapter(key_projection_rows, key_down, key_up)
    merged_value = merge_adapter(value_weight, value_down, value_up)
    merged_out = merge_adapter(output_weight, output_down, output_up)
    query_sel = jnp.take(merged_query.reshape(D, KVH, GQ), slice_group, axis=1)
    key_sel = jnp.take(merged_key.reshape(D, KVH, HD), slice_group, axis=1)
    value_sel = jnp.take(merged_value.reshape(D, KVH, HD), slice_group, axis=1)
    merged_qkv = jnp.concatenate((query_sel, key_sel, value_sel), axis=2).reshape(D, KVH * (GQ + 2 * HD))
    merged_output = jnp.take(merged_out.reshape(KVH, GQ, D), slice_group, axis=0).reshape(QD, D)
    projections = per_block_total(hidden, merged_qkv, N_DP)
    attention_output = per_block_total(context, merged_output, N_TENSOR)
    return (merged_qkv, merged_output, projections, attention_output)
```

```python
import functools

import jax
import jax.numpy as jnp
from jax import lax
from jax.experimental import pallas as pl
from jax.experimental.pallas import tpu as pltpu
from jax.sharding import PartitionSpec as P

adapter_scale_factor = 2.0
f32, bf16 = jnp.float32, jnp.bfloat16
PARAMS = dict(vmem_limit_bytes=56 * 1024 * 1024)


def swap(x, axis, mask):
    n = lax.axis_size(axis)
    return lax.ppermute(x, axis, [(i, i ^ mask) for i in range(n)])


def flipped(value, bits):
    out = 0
    for b in range(bits):
        out = out | (((value >> b) & 1) << (bits - 1 - b))
    return out


def cost(flops, nbytes):
    return pl.CostEstimate(
        flops=int(flops) // 64, bytes_accessed=int(nbytes) // 64, transcendentals=0
    )


ANY = pl.BlockSpec(memory_space=pl.ANY)
VMEM = pl.BlockSpec(memory_space=pltpu.VMEM)


def merged_t(base, down_t, up):
    update = lax.dot_general(down_t, up, (((0,), (0,)), ((), ())), preferred_element_type=f32)
    return (base.astype(f32) + adapter_scale_factor * update).astype(bf16)


def call(kernel, grid, in_specs, out_specs, out_shape, name, flops, nbytes, scratch=(), alias={}):
    return pl.pallas_call(
        kernel,
        grid_spec=pltpu.PrefetchScalarGridSpec(
            num_scalar_prefetch=1,
            grid=grid,
            in_specs=in_specs,
            out_specs=out_specs,
            scratch_shapes=scratch,
        ),
        out_shape=out_shape,
        input_output_aliases=alias,
        compiler_params=pltpu.CompilerParams(**PARAMS),
        cost_estimate=cost(flops, nbytes),
        name=name,
    )


def merge_key_value(info, key_w, value_w, key_dt, value_dt, key_u, value_u):
    def kernel(info_ref, kw, vw, kd, vd, ku, vu, mk, mv):
        mk[...] = merged_t(kw[...], kd[...], ku[...])
        mv[...] = merged_t(vw[...], vd[...], vu[...])

    shape = jax.ShapeDtypeStruct(key_w.shape, bf16)
    size = key_w.size
    return call(
        kernel, (), [VMEM] * 6, [VMEM] * 2, [shape] * 2, "merge_key_value", 256 * size, 8 * size
    )(info, key_w, value_w, key_dt, value_dt, key_u, value_u)


def group_of(s, j, i, per):
    return i[1 + (i[0] ^ s) * per + j]


def pick_qkv(info, query_w, keys, values, s, j, groups, per, after):
    rb, width = query_w.shape
    hd = keys.shape[1] // groups
    cols = width // groups
    tile = 2 * hd
    wide = cols // tile

    def kernel(info_ref, q, k, v, *rest):
        last = pl.program_id(0) == wide

        @pl.when(jnp.logical_not(last))
        def _():
            rest[-1][...] = q[...]

        @pl.when(last)
        def _():
            rest[-1][:, :hd] = k[...]
            rest[-1][:, hd:] = v[...]

    def query_at(n, i):
        return (0, group_of(s, j, i, per) * wide + jnp.minimum(n, wide - 1))

    def head_at(n, i):
        return (0, group_of(s, j, i, per))

    return call(
        kernel,
        (wide + 1,),
        [
            pl.BlockSpec((rb, tile), query_at),
            pl.BlockSpec((rb, hd), head_at),
            pl.BlockSpec((rb, hd), head_at),
        ]
        + [ANY] * len(after),
        pl.BlockSpec((rb, tile), lambda n, i: (0, n)),
        jax.ShapeDtypeStruct((rb, cols + tile), bf16),
        f"pick_qkv_{s}_{j}",
        0,
        4 * rb * (cols + tile),
    )(info, query_w, keys, values, *after)


def split_columns(info, weight, tokens, nd):
    rows, width = weight.shape
    more = tokens.shape[0]
    wide = width // nd

    def kernel(info_ref, w, t, out):
        out[0, :rows, :] = w[...]
        out[0, rows:, :] = t[...]

    return call(
        kernel,
        (nd,),
        [
            pl.BlockSpec((rows, wide), lambda d, i: (0, d)),
            pl.BlockSpec((more, wide), lambda d, i: (0, d)),
        ],
        pl.BlockSpec((1, rows + more, wide), lambda d, i: (d, 0, 0)),
        jax.ShapeDtypeStruct((nd, rows + more, wide), bf16),
        "split_columns",
        0,
        4 * (rows + more) * width,
    )(info, weight, tokens)


def pick_output(info, blocks, rb, factors, ups, s, first, count, tile, per, dpg, after):
    parts = per * dpg
    nt, rank, cb = ups.shape
    bits = nt.bit_length() - 1
    piece = min(tile, cb)
    pieces = tile // piece

    def kernel(info_ref, x, d, *rest):
        up = jnp.concatenate([u[0] for u in rest[:pieces]], axis=1)
        rest[-1][0] = merged_t(x[0], d[...], up)

    def source(l, i):
        return group_of(s, l // dpg, i, per) * dpg + l % dpg

    def up_at(p, l, c, i):
        at = (first + c) * tile + p * piece
        return (flipped((at // cb) ^ i[0], bits), 0, at % cb // piece)

    return call(
        kernel,
        (parts, count),
        [
            pl.BlockSpec((1, rb, tile), lambda l, c, i: (source(l, i), 0, first + c)),
            pl.BlockSpec((rank, rb), lambda l, c, i: (source(l, i) * (nt + 1) + nt, 0)),
        ]
        + [pl.BlockSpec((1, rank, piece), functools.partial(up_at, p)) for p in range(pieces)]
        + [ANY] * len(after),
        pl.BlockSpec((1, rb, tile), lambda l, c, i: (l, 0, c)),
        jax.ShapeDtypeStruct((parts, rb, count * tile), bf16),
        f"pick_output_{s}_{first}",
        2 * parts * rb * count * tile * rank,
        4 * parts * rb * count * tile,
    )(info, blocks, factors, *[ups] * pieces, *after)


def place_qkv(info, blocks, qkv, downs, factors, gq, per, after):
    nt, rank, cb = downs.shape
    rb, width = qkv[0][0].shape
    bits = nt.bit_length() - 1
    sources, below, depth = blocks.shape
    some = below - rb
    count = sources * some
    tile = width - gq
    each = width // tile
    wide = each - 1
    cols = per * width
    piece = min(tile, cb)
    pieces = tile // piece

    def kernel(info_ref, a, d, *refs):
        u, refs = refs[:pieces], refs[pieces:]
        full, part = refs[-2:]
        place = pl.program_id(0) // each
        last = lax.rem(pl.program_id(0), each) == wide

        def put(blocks):
            total = jnp.zeros((count, tile), f32)
            for s in range(nt):
                at = pl.ds(pl.multiple_of((info_ref[0] ^ s) * rb, rb), rb)
                full[at, :] = blocks[s]
                rows = a[:, :, at].reshape(count, rb)
                total += jnp.dot(rows, blocks[s], preferred_element_type=f32)
            part[...] = total.astype(bf16)

        for j in range(per):
            q = refs[j * nt : (j + 1) * nt]

            @pl.when(jnp.logical_and(place == j, jnp.logical_not(last)))
            def _():
                up = jnp.concatenate([x[...] for x in u], axis=1)
                put([merged_t(q[s][...], d[flipped(s, bits)], up) for s in range(nt)])

            @pl.when(jnp.logical_and(place == j, last))
            def _():
                put([x[...] for x in q])

    def column(j, n, i):
        return (0, jnp.where(n // each == j, n % each, jnp.where(n // each < j, 0, wide)))

    def up_at(p, n, i):
        at = group_of(0, n // each, i, per) * gq + jnp.minimum(n % each, wide - 1) * tile
        block = at // cb + p
        return (block // nt * (nt + 1) + flipped((block % nt) ^ i[0], bits), at % cb // piece)

    return call(
        kernel,
        (per * each,),
        [
            pl.BlockSpec((sources, some, depth), lambda n, i: (0, rb // some, 0)),
            pl.BlockSpec(downs.shape, lambda n, i: (0, 0, 0)),
        ]
        + [pl.BlockSpec((rank, piece), functools.partial(up_at, p)) for p in range(pieces)]
        + [
            pl.BlockSpec((rb, tile), functools.partial(column, j))
            for j in range(per)
            for _ in range(nt)
        ]
        + [ANY] * len(after),
        [
            pl.BlockSpec((nt * rb, tile), lambda n, i: (0, n)),
            pl.BlockSpec((count, tile), lambda n, i: (0, n)),
        ],
        [
            jax.ShapeDtypeStruct((nt * rb, cols), bf16),
            jax.ShapeDtypeStruct((count, cols), bf16),
        ],
        "place_qkv",
        2 * count * depth * cols,
        4 * depth * cols + 2 * count * cols,
    )(info, blocks, downs, *[factors] * pieces, *[x for at in qkv for x in at], *after)


def place_output(info, tokens, arrived, before, first, tile, cols, nt, after):
    parts, rb, width = arrived[0].shape
    rows, depth = tokens.shape
    each = rows // nt

    def kernel(info_ref, a, *refs):
        full, send, keep, term = refs[-4:]
        total = jnp.zeros((rows, tile), f32)
        for s in range(nt):
            for l in range(parts):
                at = pl.ds(pl.multiple_of((l * nt + (info_ref[0] ^ s)) * rb, rb), rb)
                x = refs[s][l]
                full[at, :] = x
                total += jnp.dot(a[:, at], x, preferred_element_type=f32)
        term[...] = total.astype(bf16)
        for s in range(nt):
            at = pl.ds(pl.multiple_of((info_ref[0] ^ s) * each, each), each)
            (send if s % 2 else keep)[s // 2] = term[at, :]

    operands = [info, tokens, *arrived]
    alias = {}
    if before is not None:
        alias = {len(operands): 0}
        after = [before, *after]
    half = jax.ShapeDtypeStruct((nt // 2, each, width), bf16)
    half_spec = pl.BlockSpec((nt // 2, each, tile), lambda c, i: (0, 0, c))
    return call(
        kernel,
        (width // tile,),
        [pl.BlockSpec((rows, depth), lambda c, i: (0, 0))]
        + [pl.BlockSpec((parts, rb, tile), lambda c, i: (0, 0, c))] * nt
        + [ANY] * len(after),
        [
            pl.BlockSpec((depth, tile), lambda c, i: (0, first + c)),
            half_spec,
            half_spec,
        ],
        [jax.ShapeDtypeStruct((depth, cols), bf16), half, half],
        f"place_output_{first}",
        2 * rows * depth * width,
        4 * depth * width,
        [pltpu.VMEM((rows, tile), bf16)],
        alias,
    )(*operands, *after)


def body(
    hidden,
    context,
    query_weight,
    key_projection_rows,
    value_weight,
    query_lower_factor,
    key_down,
    value_down,
    query_up,
    key_up,
    value_up,
    output_weight,
    output_down,
    output_up,
    slice_group,
):
    groups = slice_group.shape[0]
    nt, nd = lax.axis_size("tensor"), lax.axis_size("dp")
    bits = nt.bit_length() - 1
    per, dpg = groups // nt, nd // groups
    rank, cb = query_up.shape
    info = jnp.concatenate((lax.axis_index("tensor").astype(jnp.int32)[None], slice_group))

    order = list(range(nt // 2, nt)) + list(range(1, nt // 2)) + [0]

    def exchange(sent):
        return {s: swap(x, "tensor", s) if s else x for s, x in sent.items()}

    outgoing = split_columns(info, output_weight, hidden, nd)
    blocks = lax.all_to_all(outgoing, "dp", split_axis=0, concat_axis=0, tiled=True)

    keys, values = merge_key_value(
        info, key_projection_rows, value_weight, key_down.T, value_down.T, key_up, value_up
    )
    qkv = []
    for j in range(per):
        sent = {
            s: pick_qkv(info, query_weight, keys, values, s, j, groups, per, []) for s in order
        }
        got = exchange(sent)
        qkv.append([got[s] for s in range(nt)])

    factors = jnp.stack((query_up, output_up, query_lower_factor.T))[None]
    for b in reversed(range(bits)):
        factors = jnp.concatenate((factors, swap(factors, "tensor", 1 << b)))
    output_ups, query_downs = factors[:, 1], factors[:, 2]
    factors = jnp.concatenate((factors[:, 0].reshape(nt * rank, cb), output_down.T))
    factors = lax.all_gather(factors, "dp", axis=0, tiled=True)

    context_all = lax.all_gather(context, "dp", axis=0, tiled=True)

    cols = blocks.shape[2]
    tile = cols // 8
    chunks = ((0, 3), (3, 3), (6, 1), (7, 1))
    merged_output = None
    sums, early, done = [], [], []
    for n, (first, count) in enumerate(chunks):
        last = n == len(chunks) - 1
        after = done[n - 2] if n >= 2 else []
        if last:
            after = after + sums[:1]
        sent = {
            s: pick_output(
                info, blocks, output_weight.shape[0], factors, output_ups, s, first, count, tile, per, dpg, after if s else []
            )
            for s in order
        }
        got = exchange(sent)
        done.append([got[s] for s in order if s])
        if n == 1:
            merged_qkv, partial = place_qkv(
                info, blocks, qkv, query_downs, factors, query_weight.shape[1] // groups, per,
                done[0],
            )
            projections = lax.psum_scatter(partial, "dp", scatter_dimension=0, tiled=True)
        merged_output, send, keep = place_output(
            info, context_all, [got[s] for s in range(nt)], merged_output, first, tile, cols, nt,
            sums[1:-1] + early[-1:] if last else [],
        )
        for b in range(bits):
            total = (keep.astype(f32) + swap(send, "tensor", 1 << b).astype(f32)).astype(bf16)
            if b == 0:
                early.append(total)
            send, keep = total[1::2], total[0::2]
        sums.append(keep[0])
    attention_output = jnp.concatenate(sums, axis=1)
    return (merged_qkv, merged_output, projections, attention_output)


def solution(mesh):
    rows = P(("dp", "tensor"), None)
    ups = P(None, ("dp", "tensor"))
    placed = (
        P("dp", None),
        P("dp", "tensor"),
        rows,
        rows,
        rows,
        rows,
        rows,
        rows,
        ups,
        P(),
        P(),
        rows,
        rows,
        ups,
        P(),
    )
    return jax.shard_map(
        body,
        mesh=mesh,
        in_specs=placed,
        out_specs=(P("dp", "tensor"), P("tensor", "dp"), P("dp", "tensor"), P("tensor", "dp")),
        check_vma=False,
    )
```

```python
import functools

import jax
import jax.numpy as jnp
from jax import lax
from jax.experimental import pallas as pl
from jax.experimental.pallas import tpu as pltpu
from jax.sharding import PartitionSpec as P

adapter_scale_factor = 2.0
f32, bf16 = jnp.float32, jnp.bfloat16
PARAMS = dict(vmem_limit_bytes=56 * 1024 * 1024)


def total_over(axis, send, keep):
    n = lax.axis_size(axis)
    for b in range(n.bit_length() - 1):
        total = (keep.astype(f32) + swap(send, axis, 1 << b).astype(f32)).astype(bf16)
        send, keep = total[1::2], total[0::2]
    return keep[0]


def swap(x, axis, mask):
    n = lax.axis_size(axis)
    return lax.ppermute(x, axis, [(i, i ^ mask) for i in range(n)])


def flipped(value, bits):
    out = 0
    for b in range(bits):
        out = out | (((value >> b) & 1) << (bits - 1 - b))
    return out


def cost(flops, us):
    return pl.CostEstimate(flops=int(us * 1e9), bytes_accessed=0, transcendentals=0)


EST = dict(
    pack_key_value=1,
    stack_factors=1,
    split_columns=1,
    pick_output=1,
    place_qkv=1,
    place_output=200,
    pick_query=1,
    pick_query_last=300,
)
ANY = pl.BlockSpec(memory_space=pl.ANY)
VMEM = pl.BlockSpec(memory_space=pltpu.VMEM)


def merged_t(base, down_t, up):
    update = lax.dot_general(down_t, up, (((0,), (0,)), ((), ())), preferred_element_type=f32)
    return (base.astype(f32) + adapter_scale_factor * update).astype(bf16)


def call(kernel, grid, in_specs, out_specs, out_shape, name, us, scratch=(), alias={}):
    return pl.pallas_call(
        kernel,
        grid_spec=pltpu.PrefetchScalarGridSpec(
            num_scalar_prefetch=1,
            grid=grid,
            in_specs=in_specs,
            out_specs=out_specs,
            scratch_shapes=scratch,
        ),
        out_shape=out_shape,
        input_output_aliases=alias,
        compiler_params=pltpu.CompilerParams(**PARAMS),
        cost_estimate=cost(0, us),
        name=name,
    )


def group_of(s, j, i, per):
    return i[1 + (i[0] ^ s) * per + j]


def pack_key_value(info, key_w, value_w, key_dt, value_dt, key_u, value_u, nt, per):
    rb, width = key_w.shape
    hd = width // (nt * per)

    def kernel(info_ref, kw, vw, kd, vd, ku, vu, *refs):
        outs, (mk, mv) = refs[:nt], refs[nt:]
        mk[...] = merged_t(kw[...], kd[...], ku[...])
        mv[...] = merged_t(vw[...], vd[...], vu[...])
        for s in range(nt):
            for j in range(per):
                at = pl.ds(pl.multiple_of(group_of(s, j, info_ref, per) * hd, hd), hd)
                outs[s][:, (2 * j) * hd : (2 * j + 1) * hd] = mk[:, at]
                outs[s][:, (2 * j + 1) * hd : (2 * j + 2) * hd] = mv[:, at]

    return call(
        kernel,
        (),
        [VMEM] * 6,
        [VMEM] * nt,
        [jax.ShapeDtypeStruct((rb, per * 2 * hd), bf16)] * nt,
        "pack_key_value",
        EST["pack_key_value"],
        [pltpu.VMEM((rb, width), bf16)] * 2,
    )(info, key_w, value_w, key_dt, value_dt, key_u, value_u)


def pick_query(info, query_w, s, j, groups, per, us, after):
    rb, width = query_w.shape
    cols = width // groups
    steps = 4

    def kernel(info_ref, q, *refs):
        refs[-1][...] = q[...]

    return call(
        kernel,
        (steps,),
        [pl.BlockSpec((rb // steps, cols), lambda r, i: (r, group_of(s, j, i, per)))]
        + [ANY] * len(after),
        pl.BlockSpec((rb // steps, cols), lambda r, i: (r, 0)),
        jax.ShapeDtypeStruct((rb, cols), bf16),
        f"pick_query_{s}_{j}",
        us,
    )(info, query_w, *after)


def stack_factors(info, arrays, after):
    def kernel(info_ref, *refs):
        for n in range(len(arrays)):
            refs[-1][0, n] = refs[n][...]

    shape = (1, len(arrays), *arrays[0].shape)
    return call(
        kernel,
        (),
        [VMEM] * len(arrays) + [ANY] * len(after),
        VMEM,
        jax.ShapeDtypeStruct(shape, bf16),
        "stack_factors",
        EST["stack_factors"],
    )(info, *arrays, *after)


def folds(rank, rb, wide):
    return min(wide // rb, rank // 16)


def split_columns(info, weight, tokens, down_t, nd):
    rb, width = weight.shape
    more = tokens.shape[0]
    rank = down_t.shape[0]
    wide = width // nd
    parts = folds(rank, rb, wide)
    few = rank // parts
    rows = rb + more + few

    def kernel(info_ref, w, t, d, out):
        out[0, :rb, :] = w[...]
        out[0, rb : rb + more, :] = t[...]
        for p in range(parts):
            out[0, rb + more :, p * rb : (p + 1) * rb] = d[p * few : (p + 1) * few, :]

    return call(
        kernel,
        (nd,),
        [
            pl.BlockSpec((rb, wide), lambda d, i: (0, d)),
            pl.BlockSpec((more, wide), lambda d, i: (0, d)),
            pl.BlockSpec((rank, rb), lambda d, i: (0, 0)),
        ],
        pl.BlockSpec((1, rows, wide), lambda d, i: (d, 0, 0)),
        jax.ShapeDtypeStruct((nd, rows, wide), bf16),
        "split_columns",
        EST["split_columns"],
    )(info, weight, tokens, down_t)


def pick_output(info, blocks, rb, ups, s, first, count, tile, per, dpg, after):
    parts = per * dpg
    nt, rank, cb = ups.shape
    bits = nt.bit_length() - 1
    width = count * tile
    piece = min(tile, cb)
    pieces = width // piece
    steps = 2
    some = rb // steps if rb // steps % 128 == 0 else rb
    steps = rb // some
    wide = blocks.shape[2]
    parted = folds(rank, rb, wide)
    few = rank // parted
    below = blocks.shape[1] // few - 1

    def kernel(info_ref, x, *rest):
        d, up = rest[:parted], rest[parted : parted + pieces]
        down_t = jnp.concatenate([y[0] for y in d], axis=0)
        rest[-1][0] = merged_t(x[0], down_t, jnp.concatenate([u[0] for u in up], axis=1))

    def down_at(p, l, r, i):
        return (source(l, i), below, p * steps + r)

    def source(l, i):
        return group_of(s, l // dpg, i, per) * dpg + l % dpg

    def up_at(p, l, r, i):
        at = first * tile + p * piece
        return (flipped((at // cb) ^ i[0], bits), 0, at % cb // piece)

    return call(
        kernel,
        (parts, steps),
        [
            pl.BlockSpec((1, some, width), lambda l, r, i: (source(l, i), r, first // count)),
        ]
        + [pl.BlockSpec((1, few, some), functools.partial(down_at, p)) for p in range(parted)]
        + [pl.BlockSpec((1, rank, piece), functools.partial(up_at, p)) for p in range(pieces)]
        + [ANY] * len(after),
        pl.BlockSpec((1, some, width), lambda l, r, i: (l, r, 0)),
        jax.ShapeDtypeStruct((parts, rb, width), bf16),
        f"pick_output_{s}_{first}",
        EST["pick_output"],
    )(info, blocks, *[blocks] * parted, *[ups] * pieces, *after)


def place_qkv(info, blocks, hidden_rows, query, keyval, downs, factors, per, nd, after):
    nt, rank, cb = downs.shape
    rb, gq = query[0][0].shape
    bits = nt.bit_length() - 1
    sources, _, depth = blocks.shape
    some = hidden_rows
    count = sources * some
    tile = keyval[0].shape[1] // per
    wide = gq // tile
    each = wide + 1
    cols = per * each * tile
    piece = min(tile, cb)
    pieces = tile // piece

    def kernel(info_ref, a, d, *refs):
        u, refs = refs[:pieces], refs[pieces:]
        full, send, keep, term = refs[-4:]
        place = pl.program_id(0) // each
        last = lax.rem(pl.program_id(0), each) == wide

        def put(blocks):
            total = jnp.zeros((count, tile), f32)
            for s in range(nt):
                at = pl.ds(pl.multiple_of((info_ref[0] ^ s) * rb, rb), rb)
                full[at, :] = blocks[s]
                rows = a[:, :, at].reshape(count, rb)
                total += jnp.dot(rows, blocks[s], preferred_element_type=f32)
            term[...] = total.astype(bf16)
            for s in range(nd):
                at = pl.ds(pl.multiple_of((info_ref[info_ref.shape[0] - 1] ^ s) * some, some), some)
                (send if s % 2 else keep)[s // 2] = term[at, :]

        for j in range(per):
            q = refs[j * nt : (j + 1) * nt]

            @pl.when(jnp.logical_and(place == j, jnp.logical_not(last)))
            def _():
                up = jnp.concatenate([x[...] for x in u], axis=1)
                put([merged_t(q[s][...], d[flipped(s, bits)], up) for s in range(nt)])

        @pl.when(last)
        def _():
            put([x[...] for x in refs[per * nt : (per + 1) * nt]])

    def column(j, n, i):
        k, w = n // each, jnp.minimum(n % each, wide - 1)
        return (0, jnp.where(k == j, w, jnp.where(k < j, 0, wide - 1)))

    def up_at(p, n, i):
        at = group_of(0, n // each, i, per) * gq + jnp.minimum(n % each, wide - 1) * tile
        block = at // cb + p
        return (block // nt * nt + flipped((block % nt) ^ i[0], bits), at % cb // piece)

    half = jax.ShapeDtypeStruct((nd // 2, count // nd, cols), bf16)
    half_spec = pl.BlockSpec((nd // 2, count // nd, tile), lambda n, i: (0, 0, n))
    return call(
        kernel,
        (per * each,),
        [
            pl.BlockSpec((sources, some, depth), lambda n, i: (0, rb // some, 0)),
            pl.BlockSpec(downs.shape, lambda n, i: (0, 0, 0)),
        ]
        + [pl.BlockSpec((rank, piece), functools.partial(up_at, p)) for p in range(pieces)]
        + [
            pl.BlockSpec((rb, tile), functools.partial(column, j))
            for j in range(per)
            for _ in range(nt)
        ]
        + [pl.BlockSpec((rb, tile), lambda n, i: (0, n // each))] * nt
        + [ANY] * len(after),
        [
            pl.BlockSpec((nt * rb, tile), lambda n, i: (0, n)),
            half_spec,
            half_spec,
        ],
        [jax.ShapeDtypeStruct((nt * rb, cols), bf16), half, half],
        "place_qkv",
        EST["place_qkv"],
        [pltpu.VMEM((count, tile), bf16)],
    )(info, blocks, downs, *[factors] * pieces, *[x for at in query for x in at], *keyval, *after)


def place_output(info, tokens, arrived, before, first, tile, cols, nt, after):
    parts, rb, width = arrived[0].shape
    rows, depth = tokens.shape
    each = rows // nt

    def kernel(info_ref, a, *refs):
        full, send, keep, term = refs[-4:]
        total = jnp.zeros((rows, tile), f32)
        for s in range(nt):
            for l in range(parts):
                at = pl.ds(pl.multiple_of((l * nt + (info_ref[0] ^ s)) * rb, rb), rb)
                x = refs[s][l]
                full[at, :] = x
                total += jnp.dot(a[:, at], x, preferred_element_type=f32)
        term[...] = total.astype(bf16)
        for s in range(nt):
            at = pl.ds(pl.multiple_of((info_ref[0] ^ s) * each, each), each)
            (send if s % 2 else keep)[s // 2] = term[at, :]

    operands = [info, tokens, *arrived]
    alias = {}
    if before is not None:
        alias = {len(operands): 0}
        after = [before, *after]
    half = jax.ShapeDtypeStruct((nt // 2, each, width), bf16)
    half_spec = pl.BlockSpec((nt // 2, each, tile), lambda c, i: (0, 0, c))
    return call(
        kernel,
        (width // tile,),
        [pl.BlockSpec((rows, depth), lambda c, i: (0, 0))]
        + [pl.BlockSpec((parts, rb, tile), lambda c, i: (0, 0, c))] * nt
        + [ANY] * len(after),
        [
            pl.BlockSpec((depth, tile), lambda c, i: (0, first + c)),
            half_spec,
            half_spec,
        ],
        [jax.ShapeDtypeStruct((depth, cols), bf16), half, half],
        f"place_output_{first}",
        EST["place_output"],
        [pltpu.VMEM((rows, tile), bf16)],
        alias,
    )(*operands, *after)


def body(
    hidden,
    context,
    query_weight,
    key_projection_rows,
    value_weight,
    query_lower_factor,
    key_down,
    value_down,
    query_up,
    key_up,
    value_up,
    output_weight,
    output_down,
    output_up,
    slice_group,
):
    groups = slice_group.shape[0]
    nt, nd = lax.axis_size("tensor"), lax.axis_size("dp")
    bits = nt.bit_length() - 1
    per, dpg = groups // nt, nd // groups
    rank, cb = query_up.shape
    place = [lax.axis_index(axis).astype(jnp.int32)[None] for axis in ("tensor", "dp")]
    info = jnp.concatenate((place[0], slice_group, place[1]))

    order = list(range(nt // 2, nt)) + list(range(1, nt // 2)) + [0]

    def exchange(sent):
        return {s: swap(x, "tensor", s) if s else x for s, x in sent.items()}

    keyval = pack_key_value(
        info, key_projection_rows, value_weight, key_down.T, value_down.T, key_up, value_up, nt, per
    )
    got = exchange({s: keyval[s] for s in order})
    keyval = [got[s] for s in range(nt)]
    outgoing = split_columns(info, output_weight, hidden, output_down.T, nd)
    blocks = lax.all_to_all(outgoing, "dp", split_axis=0, concat_axis=0, tiled=True)

    query = []
    for j in range(per):
        sent = {}
        for s in order:
            late = j == 0 and s == 1
            us = EST["pick_query_last" if late else "pick_query"]
            after = keyval[1:] if late else []
            sent[s] = pick_query(info, query_weight, s, j, groups, per, us, after)
        got = exchange(sent)
        query.append([got[s] for s in range(nt)])

    factors = stack_factors(info, (query_up, output_up, query_lower_factor.T), [])
    for b in reversed(range(bits)):
        factors = jnp.concatenate((factors, swap(factors, "tensor", 1 << b)))
    output_ups, query_downs = factors[:, 1], factors[:, 2]
    query_ups = lax.all_gather(factors[:, 0].reshape(nt * rank, cb), "dp", axis=0, tiled=True)

    context_all = lax.all_gather(context, "dp", axis=0, tiled=True)

    cols = blocks.shape[2]
    tile = cols // 8
    chunks = ((0, 3), (3, 3), (6, 1), (7, 1))
    merged_output = None
    sums, done = [], []
    for n, (first, count) in enumerate(chunks):
        last = n == len(chunks) - 1
        after = done[n - 2] if n >= 2 else []
        sent = {
            s: pick_output(
                info, blocks, output_weight.shape[0], output_ups, s, first, count, tile, per, dpg, after if s else []
            )
            for s in order
        }
        got = exchange(sent)
        done.append([got[s] for s in order if s])
        if n == 0:
            merged_qkv, *partial = place_qkv(
                info, blocks, hidden.shape[0], query, keyval, query_downs, query_ups, per, nd, done[0]
            )
            projections = total_over("dp", *partial)
        merged_output, send, keep = place_output(
            info, context_all, [got[s] for s in range(nt)], merged_output, first, tile, cols, nt,
            partial[:1] if n == 1 else sums[:-1] + [projections] if last else [],
        )
        sums.append(total_over("tensor", send, keep))
    attention_output = jnp.concatenate(sums, axis=1)
    return (merged_qkv, merged_output, projections, attention_output)


def solution(mesh):
    rows = P(("dp", "tensor"), None)
    ups = P(None, ("dp", "tensor"))
    placed = (
        P("dp", None),
        P("dp", "tensor"),
        rows,
        rows,
        rows,
        rows,
        rows,
        rows,
        ups,
        P(),
        P(),
        rows,
        rows,
        ups,
        P(),
    )
    return jax.shard_map(
        body,
        mesh=mesh,
        in_specs=placed,
        out_specs=(P("dp", "tensor"), P("tensor", "dp"), P("dp", "tensor"), P("tensor", "dp")),
        check_vma=False,
    )
```

```python
import functools

import jax
import jax.numpy as jnp
from jax import lax
from jax.experimental import pallas as pl
from jax.experimental.pallas import tpu as pltpu
from jax.sharding import PartitionSpec as P

adapter_scale_factor = 2.0
f32, bf16 = jnp.float32, jnp.bfloat16
PARAMS = dict(vmem_limit_bytes=56 * 1024 * 1024)


def total_over(axis, send, keep):
    n = lax.axis_size(axis)
    for b in range(n.bit_length() - 1):
        total = (keep.astype(f32) + swap(send, axis, 1 << b).astype(f32)).astype(bf16)
        send, keep = total[1::2], total[0::2]
    return keep[0]


def swap(x, axis, mask):
    n = lax.axis_size(axis)
    return lax.ppermute(x, axis, [(i, i ^ mask) for i in range(n)])


def cost(flops, us):
    return pl.CostEstimate(flops=int(us * 1e9), bytes_accessed=0, transcendentals=0)


EST = dict(
    pack_key_value=1,
    split_columns=1,
    pick_output=1,
    place_qkv=1,
    place_output=200,
    pick_query=1,
    pick_query_last=300,
)
ANY = pl.BlockSpec(memory_space=pl.ANY)
VMEM = pl.BlockSpec(memory_space=pltpu.VMEM)


def merged_t(base, down_t, up):
    update = lax.dot_general(down_t, up, (((0,), (0,)), ((), ())), preferred_element_type=f32)
    return (base.astype(f32) + adapter_scale_factor * update).astype(bf16)


def call(kernel, grid, in_specs, out_specs, out_shape, name, us, scratch=(), alias={}):
    return pl.pallas_call(
        kernel,
        grid_spec=pltpu.PrefetchScalarGridSpec(
            num_scalar_prefetch=1,
            grid=grid,
            in_specs=in_specs,
            out_specs=out_specs,
            scratch_shapes=scratch,
        ),
        out_shape=out_shape,
        input_output_aliases=alias,
        compiler_params=pltpu.CompilerParams(**PARAMS),
        cost_estimate=cost(0, us),
        name=name,
    )


def group_of(s, j, i, per):
    return i[1 + (i[0] ^ s) * per + j]


def pack_key_value(info, key_w, value_w, key_dt, value_dt, key_u, value_u, riders, nt, per):
    rb, width = key_w.shape
    hd = width // (nt * per)
    some, wide = riders[0].shape
    count = len(riders)

    def kernel(info_ref, kw, vw, kd, vd, ku, vu, *refs):
        outs, (mk, mv) = refs[count : count + nt], refs[count + nt :]
        mk[...] = merged_t(kw[...], kd[...], ku[...])
        mv[...] = merged_t(vw[...], vd[...], vu[...])
        for s in range(nt):
            for j in range(per):
                at = pl.ds(pl.multiple_of(group_of(s, j, info_ref, per) * hd, hd), hd)
                outs[s][:rb, (2 * j) * hd : (2 * j + 1) * hd] = mk[:, at]
                outs[s][:rb, (2 * j + 1) * hd : (2 * j + 2) * hd] = mv[:, at]
            for n in range(count):
                outs[s][rb + n * some : rb + (n + 1) * some, :wide] = refs[n][...]

    return call(
        kernel,
        (),
        [VMEM] * (6 + count),
        [VMEM] * nt,
        [jax.ShapeDtypeStruct((rb + count * some, per * 2 * hd), bf16)] * nt,
        "pack_key_value",
        EST["pack_key_value"],
        [pltpu.VMEM((rb, width), bf16)] * 2,
    )(info, key_w, value_w, key_dt, value_dt, key_u, value_u, *riders)


def pick_query(info, query_w, s, j, groups, per, us, after):
    rb, width = query_w.shape
    cols = width // groups
    steps = 4

    def kernel(info_ref, q, *refs):
        refs[-1][...] = q[...]

    return call(
        kernel,
        (steps,),
        [pl.BlockSpec((rb // steps, cols), lambda r, i: (r, group_of(s, j, i, per)))]
        + [ANY] * len(after),
        pl.BlockSpec((rb // steps, cols), lambda r, i: (r, 0)),
        jax.ShapeDtypeStruct((rb, cols), bf16),
        f"pick_query_{s}_{j}",
        us,
    )(info, query_w, *after)


def folds(rank, rb, wide):
    return min(wide // rb, rank // 16)


def split_columns(info, weight, tokens, factors, nd):
    rb, width = weight.shape
    more = tokens.shape[0]
    rank = factors[0].shape[0]
    wide = width // nd
    parts = folds(rank, rb, wide)
    few = rank // parts
    rows = rb + more + len(factors) * few

    def kernel(info_ref, w, t, *refs):
        out = refs[-1]
        out[0, :rb, :] = w[...]
        out[0, rb : rb + more, :] = t[...]
        for n in range(len(factors)):
            at = rb + more + n * few
            for p in range(parts):
                out[0, at : at + few, p * rb : (p + 1) * rb] = refs[n][p * few : (p + 1) * few, :]

    return call(
        kernel,
        (nd,),
        [
            pl.BlockSpec((rb, wide), lambda d, i: (0, d)),
            pl.BlockSpec((more, wide), lambda d, i: (0, d)),
        ]
        + [pl.BlockSpec((rank, rb), lambda d, i: (0, 0))] * len(factors),
        pl.BlockSpec((1, rows, wide), lambda d, i: (d, 0, 0)),
        jax.ShapeDtypeStruct((nd, rows, wide), bf16),
        "split_columns",
        EST["split_columns"],
    )(info, weight, tokens, *factors)


def pick_output(info, blocks, rb, ups, s, first, count, tile, per, dpg, after):
    parts = per * dpg
    nt, rank, cb = ups.shape
    width = count * tile
    piece = min(tile, cb)
    pieces = width // piece
    parted = folds(rank, rb, blocks.shape[2])
    few = rank // parted
    end = blocks.shape[1] // few
    more = 0 if first else rank

    def kernel(info_ref, x, *refs):
        d, r = refs[:parted], refs[parted : 2 * parted]
        up, out = refs[2 * parted : 2 * parted + pieces], refs[-1]
        down_t = jnp.concatenate([y[0] for y in d], axis=0)
        out[0, :rb, :] = merged_t(x[0], down_t, jnp.concatenate([u[0] for u in up], axis=1))
        if more:
            for p in range(parted):
                out[0, rb + p * few : rb + (p + 1) * few, :cb] = r[p][0]

    def source(l, i):
        return group_of(s, l // dpg, i, per) * dpg + l % dpg

    def factor_at(row, p, l, i):
        return (source(l, i), row, p)

    def up_at(p, l, i):
        at = first * tile + p * piece
        return ((at // cb) ^ i[0], 0, at % cb // piece)

    return call(
        kernel,
        (parts,),
        [pl.BlockSpec((1, rb, width), lambda l, i: (source(l, i), 0, first // count))]
        + [
            pl.BlockSpec((1, few, cb), functools.partial(factor_at, row, p))
            for row in (end - 2, end - 1)
            for p in range(parted)
        ]
        + [pl.BlockSpec((1, rank, piece), functools.partial(up_at, p)) for p in range(pieces)]
        + [ANY] * len(after),
        pl.BlockSpec((1, rb + more, width), lambda l, i: (l, 0, 0)),
        jax.ShapeDtypeStruct((parts, rb + more, width), bf16),
        f"pick_output_{s}_{first}",
        EST["pick_output"],
    )(info, blocks, *[blocks] * (2 * parted), *[ups] * pieces, *after)


def place_qkv(info, blocks, hidden_rows, query, keyval, downs, ups, per, dpg, nd):
    nt, rank, cb = downs.shape
    rb, gq = query[0][0].shape
    sources, _, depth = blocks.shape
    some = hidden_rows
    count = sources * some
    tile = keyval[0].shape[1] // per
    wide = gq // tile
    each = wide + 1
    cols = per * each * tile
    piece = min(tile, cb)
    pieces = tile // piece

    def kernel(info_ref, a, d, *refs):
        u, refs = refs[:pieces], refs[pieces:]
        full, send, keep, term = refs[-4:]
        place = pl.program_id(0) // each
        last = lax.rem(pl.program_id(0), each) == wide

        def put(blocks):
            total = jnp.zeros((count, tile), f32)
            for s in range(nt):
                at = pl.ds(pl.multiple_of((info_ref[0] ^ s) * rb, rb), rb)
                full[at, :] = blocks[s]
                rows = a[:, :, at].reshape(count, rb)
                total += jnp.dot(rows, blocks[s], preferred_element_type=f32)
            term[...] = total.astype(bf16)
            for s in range(nd):
                at = pl.ds(pl.multiple_of((info_ref[info_ref.shape[0] - 1] ^ s) * some, some), some)
                (send if s % 2 else keep)[s // 2] = term[at, :]

        for j in range(per):
            q = refs[j * nt : (j + 1) * nt]

            @pl.when(jnp.logical_and(place == j, jnp.logical_not(last)))
            def _():
                up = jnp.concatenate([x[0, 0] for x in u], axis=1)
                put([merged_t(q[s][...], d[s], up) for s in range(nt)])

        @pl.when(last)
        def _():
            put([x[...] for x in refs[per * nt : (per + 1) * nt]])

    def column(j, n, i):
        k, w = n // each, jnp.minimum(n % each, wide - 1)
        return (0, jnp.where(k == j, w, jnp.where(k < j, 0, wide - 1)))

    def up_at(p, n, i):
        at = jnp.minimum(n % each, wide - 1) * tile
        block = at // cb + p
        return ((block % nt) ^ i[0], (n // each) * dpg + block // nt, 0, at % cb // piece)

    half = jax.ShapeDtypeStruct((nd // 2, count // nd, cols), bf16)
    half_spec = pl.BlockSpec((nd // 2, count // nd, tile), lambda n, i: (0, 0, n))
    return call(
        kernel,
        (per * each,),
        [
            pl.BlockSpec((sources, some, depth), lambda n, i: (0, rb // some, 0)),
            pl.BlockSpec(downs.shape, lambda n, i: (0, 0, 0)),
        ]
        + [pl.BlockSpec((1, 1, rank, piece), functools.partial(up_at, p)) for p in range(pieces)]
        + [
            pl.BlockSpec((rb, tile), functools.partial(column, j))
            for j in range(per)
            for _ in range(nt)
        ]
        + [pl.BlockSpec((rb, tile), lambda n, i: (0, n // each))] * nt,
        [
            pl.BlockSpec((nt * rb, tile), lambda n, i: (0, n)),
            half_spec,
            half_spec,
        ],
        [jax.ShapeDtypeStruct((nt * rb, cols), bf16), half, half],
        "place_qkv",
        EST["place_qkv"],
        [pltpu.VMEM((count, tile), bf16)],
    )(info, blocks, downs, *[ups] * pieces, *[x for at in query for x in at], *keyval)


def place_output(info, tokens, arrived, rb, before, first, tile, cols, nt, after):
    parts, _, width = arrived[0].shape
    rows, depth = tokens.shape
    each = rows // nt

    def kernel(info_ref, a, *refs):
        full, send, keep, term = refs[-4:]
        total = jnp.zeros((rows, tile), f32)
        for s in range(nt):
            for l in range(parts):
                at = pl.ds(pl.multiple_of((l * nt + (info_ref[0] ^ s)) * rb, rb), rb)
                x = refs[s][l]
                full[at, :] = x
                total += jnp.dot(a[:, at], x, preferred_element_type=f32)
        term[...] = total.astype(bf16)
        for s in range(nt):
            at = pl.ds(pl.multiple_of((info_ref[0] ^ s) * each, each), each)
            (send if s % 2 else keep)[s // 2] = term[at, :]

    operands = [info, tokens, *arrived]
    alias = {}
    if before is not None:
        alias = {len(operands): 0}
        after = [before, *after]
    half = jax.ShapeDtypeStruct((nt // 2, each, width), bf16)
    half_spec = pl.BlockSpec((nt // 2, each, tile), lambda c, i: (0, 0, c))
    return call(
        kernel,
        (width // tile,),
        [pl.BlockSpec((rows, depth), lambda c, i: (0, 0))]
        + [pl.BlockSpec((parts, rb, tile), lambda c, i: (0, 0, c))] * nt
        + [ANY] * len(after),
        [
            pl.BlockSpec((depth, tile), lambda c, i: (0, first + c)),
            half_spec,
            half_spec,
        ],
        [jax.ShapeDtypeStruct((depth, cols), bf16), half, half],
        f"place_output_{first}",
        EST["place_output"],
        [pltpu.VMEM((rows, tile), bf16)],
        alias,
    )(*operands, *after)


def body(
    hidden,
    context,
    query_weight,
    key_projection_rows,
    value_weight,
    query_lower_factor,
    key_down,
    value_down,
    query_up,
    key_up,
    value_up,
    output_weight,
    output_down,
    output_up,
    slice_group,
):
    groups = slice_group.shape[0]
    nt, nd = lax.axis_size("tensor"), lax.axis_size("dp")
    per, dpg = groups // nt, nd // groups
    rank, cb = query_up.shape
    place = [lax.axis_index(axis).astype(jnp.int32)[None] for axis in ("tensor", "dp")]
    info = jnp.concatenate((place[0], slice_group, place[1]))

    order = list(range(nt // 2, nt)) + list(range(1, nt // 2)) + [0]

    def exchange(sent):
        return {s: swap(x, "tensor", s) if s else x for s, x in sent.items()}

    keyval = pack_key_value(
        info,
        key_projection_rows,
        value_weight,
        key_down.T,
        value_down.T,
        key_up,
        value_up,
        (output_up, query_lower_factor.T),
        nt,
        per,
    )
    got = exchange({s: keyval[s] for s in order})
    keyval = [got[s] for s in range(nt)]
    rb = query_weight.shape[0]
    output_ups = jnp.stack([x[rb : rb + rank, :cb] for x in keyval])
    query_downs = jnp.stack([x[rb + rank :, :rb] for x in keyval])
    outgoing = split_columns(info, output_weight, hidden, (output_down.T, query_up), nd)
    blocks = lax.all_to_all(outgoing, "dp", split_axis=0, concat_axis=0, tiled=True)

    query = []
    for j in range(per):
        sent = {}
        for s in order:
            late = j == 0 and s == 1
            us = EST["pick_query_last" if late else "pick_query"]
            after = keyval[1:] if late else []
            sent[s] = pick_query(info, query_weight, s, j, groups, per, us, after)
        got = exchange(sent)
        query.append([got[s] for s in range(nt)])

    context_all = lax.all_gather(context, "dp", axis=0, tiled=True)

    cols = blocks.shape[2]
    tile = cols // 8
    chunks = ((0, 3), (3, 3), (6, 1), (7, 1))
    merged_output = None
    sums, done = [], []
    for n, (first, count) in enumerate(chunks):
        last = n == len(chunks) - 1
        sent = {}
        for s in order:
            after = []
            if s and n == 0:
                after = query[0][1:] + (query[-1][1:] if s == 1 else [])
            elif s and last:
                after = picked
            elif s and n >= 2:
                after = done[n - 2]
            sent[s] = pick_output(
                info, blocks, rb, output_ups, s, first, count, tile, per, dpg, after
            )
        picked = [sent[s] for s in order if s]
        got = exchange(sent)
        done.append([got[s] for s in order if s])
        if n == 0:
            query_ups = jnp.stack([got[s][:, rb:, :cb] for s in range(nt)])
            merged_qkv, *partial = place_qkv(
                info, blocks, hidden.shape[0], query, keyval, query_downs, query_ups, per, dpg, nd
            )
            projections = total_over("dp", *partial)
        merged_output, send, keep = place_output(
            info, context_all, [got[s] for s in range(nt)], rb, merged_output, first, tile, cols, nt,
            partial[:1] if n == 1 else sums[:-1] + [projections] if last else [],
        )
        sums.append(total_over("tensor", send, keep))
    attention_output = jnp.concatenate(sums, axis=1)
    return (merged_qkv, merged_output, projections, attention_output)


def solution(mesh):
    rows = P(("dp", "tensor"), None)
    ups = P(None, ("dp", "tensor"))
    placed = (
        P("dp", None),
        P("dp", "tensor"),
        rows,
        rows,
        rows,
        rows,
        rows,
        rows,
        ups,
        P(),
        P(),
        rows,
        rows,
        ups,
        P(),
    )
    return jax.shard_map(
        body,
        mesh=mesh,
        in_specs=placed,
        out_specs=(P("dp", "tensor"), P("tensor", "dp"), P("dp", "tensor"), P("tensor", "dp")),
        check_vma=False,
    )
```

```python
import functools

import jax
import jax.numpy as jnp
from jax import lax
from jax.experimental import pallas as pl
from jax.experimental.pallas import tpu as pltpu
from jax.sharding import PartitionSpec as P

adapter_scale_factor = 2.0
f32, bf16 = jnp.float32, jnp.bfloat16
PARAMS = dict(vmem_limit_bytes=56 * 1024 * 1024)


def total_over(axis, send, keep):
    n = lax.axis_size(axis)
    for b in range(n.bit_length() - 1):
        total = (keep.astype(f32) + swap(send, axis, 1 << b).astype(f32)).astype(bf16)
        send, keep = total[1::2], total[0::2]
    return keep[0]


def swap(x, axis, mask):
    n = lax.axis_size(axis)
    return lax.ppermute(x, axis, [(i, i ^ mask) for i in range(n)])


def cost(flops, us):
    return pl.CostEstimate(flops=int(us * 1e9), bytes_accessed=0, transcendentals=0)


EST = dict(
    pack_key_value=1,
    split_columns=1,
    pick_output=1,
    place_qkv=1,
    place_output=200,
    pick_query=1,
    pick_query_last=300,
)
ANY = pl.BlockSpec(memory_space=pl.ANY)
VMEM = pl.BlockSpec(memory_space=pltpu.VMEM)


def merged_t(base, down_t, up):
    update = lax.dot_general(down_t, up, (((0,), (0,)), ((), ())), preferred_element_type=f32)
    return (base.astype(f32) + adapter_scale_factor * update).astype(bf16)


def call(kernel, grid, in_specs, out_specs, out_shape, name, us, scratch=(), alias={}):
    return pl.pallas_call(
        kernel,
        grid_spec=pltpu.PrefetchScalarGridSpec(
            num_scalar_prefetch=1,
            grid=grid,
            in_specs=in_specs,
            out_specs=out_specs,
            scratch_shapes=scratch,
        ),
        out_shape=out_shape,
        input_output_aliases=alias,
        compiler_params=pltpu.CompilerParams(**PARAMS),
        cost_estimate=cost(0, us),
        name=name,
    )


def group_of(s, j, i, per):
    return i[1 + (i[0] ^ s) * per + j]


def pack_key_value(info, key_w, value_w, key_dt, value_dt, key_u, value_u, riders, nt, per):
    rb, width = key_w.shape
    hd = width // (nt * per)
    some, wide = riders[0].shape
    count = len(riders)

    def kernel(info_ref, kw, vw, kd, vd, ku, vu, *refs):
        outs, (mk, mv) = refs[count : count + nt], refs[count + nt :]
        mk[...] = merged_t(kw[...], kd[...], ku[...])
        mv[...] = merged_t(vw[...], vd[...], vu[...])
        for s in range(nt):
            for j in range(per):
                at = pl.ds(pl.multiple_of(group_of(s, j, info_ref, per) * hd, hd), hd)
                outs[s][:rb, (2 * j) * hd : (2 * j + 1) * hd] = mk[:, at]
                outs[s][:rb, (2 * j + 1) * hd : (2 * j + 2) * hd] = mv[:, at]
            for n in range(count):
                outs[s][rb + n * some : rb + (n + 1) * some, :wide] = refs[n][...]

    return call(
        kernel,
        (),
        [VMEM] * (6 + count),
        [VMEM] * nt,
        [jax.ShapeDtypeStruct((rb + count * some, per * 2 * hd), bf16)] * nt,
        "pack_key_value",
        EST["pack_key_value"],
        [pltpu.VMEM((rb, width), bf16)] * 2,
    )(info, key_w, value_w, key_dt, value_dt, key_u, value_u, *riders)


def pick_query(info, query_w, s, j, groups, per, us, after):
    rb, width = query_w.shape
    cols = width // groups
    steps = 4

    def kernel(info_ref, q, *refs):
        refs[-1][...] = q[...]

    return call(
        kernel,
        (steps,),
        [pl.BlockSpec((rb // steps, cols), lambda r, i: (r, group_of(s, j, i, per)))]
        + [ANY] * len(after),
        pl.BlockSpec((rb // steps, cols), lambda r, i: (r, 0)),
        jax.ShapeDtypeStruct((rb, cols), bf16),
        f"pick_query_{s}_{j}",
        us,
    )(info, query_w, *after)


def folds(rank, rb, wide):
    return min(wide // rb, rank // 16)


def split_columns(info, weight, tokens, factors, nd):
    rb, width = weight.shape
    more = tokens.shape[0]
    rank = factors[0].shape[0]
    wide = width // nd
    parts = folds(rank, rb, wide)
    few = rank // parts
    rows = rb + more + len(factors) * few

    def kernel(info_ref, w, t, *refs):
        out = refs[-1]
        out[0, :rb, :] = w[...]
        out[0, rb : rb + more, :] = t[...]
        for n in range(len(factors)):
            at = rb + more + n * few
            for p in range(parts):
                out[0, at : at + few, p * rb : (p + 1) * rb] = refs[n][p * few : (p + 1) * few, :]

    return call(
        kernel,
        (nd,),
        [
            pl.BlockSpec((rb, wide), lambda d, i: (0, d)),
            pl.BlockSpec((more, wide), lambda d, i: (0, d)),
        ]
        + [pl.BlockSpec((rank, rb), lambda d, i: (0, 0))] * len(factors),
        pl.BlockSpec((1, rows, wide), lambda d, i: (d, 0, 0)),
        jax.ShapeDtypeStruct((nd, rows, wide), bf16),
        "split_columns",
        EST["split_columns"],
    )(info, weight, tokens, *factors)


def pick_output(info, blocks, rb, ups, s, first, count, tile, per, dpg, after):
    parts = per * dpg
    nt, rank, cb = ups.shape
    width = count * tile
    piece = min(tile, cb)
    pieces = width // piece
    parted = folds(rank, rb, blocks.shape[2])
    few = rank // parted
    end = blocks.shape[1] // few
    more = 0 if first else rank

    def kernel(info_ref, x, *refs):
        d, r = refs[:parted], refs[parted : 2 * parted]
        up, out = refs[2 * parted : 2 * parted + pieces], refs[-1]
        down_t = jnp.concatenate([y[0] for y in d], axis=0)
        out[0, :rb, :] = merged_t(x[0], down_t, jnp.concatenate([u[0] for u in up], axis=1))
        if more:
            for p in range(parted):
                out[0, rb + p * few : rb + (p + 1) * few, :cb] = r[p][0]

    def source(l, i):
        return group_of(s, l // dpg, i, per) * dpg + l % dpg

    def factor_at(row, p, l, i):
        return (source(l, i), row, p)

    def up_at(p, l, i):
        at = first * tile + p * piece
        return ((at // cb) ^ i[0], 0, at % cb // piece)

    return call(
        kernel,
        (parts,),
        [pl.BlockSpec((1, rb, width), lambda l, i: (source(l, i), 0, first // count))]
        + [
            pl.BlockSpec((1, few, cb), functools.partial(factor_at, row, p))
            for row in (end - 2, end - 1)
            for p in range(parted)
        ]
        + [pl.BlockSpec((1, rank, piece), functools.partial(up_at, p)) for p in range(pieces)]
        + [ANY] * len(after),
        pl.BlockSpec((1, rb + more, width), lambda l, i: (l, 0, 0)),
        jax.ShapeDtypeStruct((parts, rb + more, width), bf16),
        f"pick_output_{s}_{first}",
        EST["pick_output"],
    )(info, blocks, *[blocks] * (2 * parted), *[ups] * pieces, *after)


def place_qkv(info, blocks, hidden_rows, query, keyval, downs, ups, per, dpg, nd):
    nt, rank, cb = downs.shape
    rb, gq = query[0][0].shape
    sources, _, depth = blocks.shape
    some = hidden_rows
    count = sources * some
    tile = keyval[0].shape[1] // per
    wide = gq // tile
    each = wide + 1
    cols = per * each * tile
    piece = min(tile, cb)
    pieces = tile // piece

    def kernel(info_ref, a, d, *refs):
        u, refs = refs[:pieces], refs[pieces:]
        full, send, keep, term = refs[-4:]
        place = pl.program_id(0) // each
        last = lax.rem(pl.program_id(0), each) == wide

        def put(blocks):
            total = jnp.zeros((count, tile), f32)
            for s in range(nt):
                at = pl.ds(pl.multiple_of((info_ref[0] ^ s) * rb, rb), rb)
                full[at, :] = blocks[s]
                rows = a[:, :, at].reshape(count, rb)
                total += jnp.dot(rows, blocks[s], preferred_element_type=f32)
            term[...] = total.astype(bf16)
            for s in range(nd):
                at = pl.ds(pl.multiple_of((info_ref[info_ref.shape[0] - 1] ^ s) * some, some), some)
                (send if s % 2 else keep)[s // 2] = term[at, :]

        for j in range(per):
            q = refs[j * nt : (j + 1) * nt]

            @pl.when(jnp.logical_and(place == j, jnp.logical_not(last)))
            def _():
                up = jnp.concatenate([x[0, 0] for x in u], axis=1)
                put([merged_t(q[s][...], d[s], up) for s in range(nt)])

        @pl.when(last)
        def _():
            put([x[...] for x in refs[per * nt : (per + 1) * nt]])

    def column(j, n, i):
        k, w = n // each, jnp.minimum(n % each, wide - 1)
        return (0, jnp.where(k == j, w, jnp.where(k < j, 0, wide - 1)))

    def up_at(p, n, i):
        at = jnp.minimum(n % each, wide - 1) * tile
        block = at // cb + p
        return ((block % nt) ^ i[0], (n // each) * dpg + block // nt, 0, at % cb // piece)

    half = jax.ShapeDtypeStruct((nd // 2, count // nd, cols), bf16)
    half_spec = pl.BlockSpec((nd // 2, count // nd, tile), lambda n, i: (0, 0, n))
    return call(
        kernel,
        (per * each,),
        [
            pl.BlockSpec((sources, some, depth), lambda n, i: (0, rb // some, 0)),
            pl.BlockSpec(downs.shape, lambda n, i: (0, 0, 0)),
        ]
        + [pl.BlockSpec((1, 1, rank, piece), functools.partial(up_at, p)) for p in range(pieces)]
        + [
            pl.BlockSpec((rb, tile), functools.partial(column, j))
            for j in range(per)
            for _ in range(nt)
        ]
        + [pl.BlockSpec((rb, tile), lambda n, i: (0, n // each))] * nt,
        [
            pl.BlockSpec((nt * rb, tile), lambda n, i: (0, n)),
            half_spec,
            half_spec,
        ],
        [jax.ShapeDtypeStruct((nt * rb, cols), bf16), half, half],
        "place_qkv",
        EST["place_qkv"],
        [pltpu.VMEM((count, tile), bf16)],
    )(info, blocks, downs, *[ups] * pieces, *[x for at in query for x in at], *keyval)


def place_output(info, tokens, arrived, rb, before, first, tile, cols, nt, after):
    parts, _, width = arrived[0].shape
    rows, depth = tokens.shape
    each = rows // nt

    def kernel(info_ref, a, *refs):
        full, send, keep, term = refs[-4:]
        total = jnp.zeros((rows, tile), f32)
        for s in range(nt):
            for l in range(parts):
                at = pl.ds(pl.multiple_of((l * nt + (info_ref[0] ^ s)) * rb, rb), rb)
                x = refs[s][l]
                full[at, :] = x
                total += jnp.dot(a[:, at], x, preferred_element_type=f32)
        term[...] = total.astype(bf16)
        for s in range(nt):
            at = pl.ds(pl.multiple_of((info_ref[0] ^ s) * each, each), each)
            (send if s % 2 else keep)[s // 2] = term[at, :]

    operands = [info, tokens, *arrived]
    alias = {}
    if before is not None:
        alias = {len(operands): 0}
        after = [before, *after]
    half = jax.ShapeDtypeStruct((nt // 2, each, width), bf16)
    half_spec = pl.BlockSpec((nt // 2, each, tile), lambda c, i: (0, 0, c))
    return call(
        kernel,
        (width // tile,),
        [pl.BlockSpec((rows, depth), lambda c, i: (0, 0))]
        + [pl.BlockSpec((parts, rb, tile), lambda c, i: (0, 0, c))] * nt
        + [ANY] * len(after),
        [
            pl.BlockSpec((depth, tile), lambda c, i: (0, first // tile + c)),
            half_spec,
            half_spec,
        ],
        [jax.ShapeDtypeStruct((depth, cols), bf16), half, half],
        f"place_output_{first}",
        EST["place_output"],
        [pltpu.VMEM((rows, tile), bf16)],
        alias,
    )(*operands, *after)


def body(
    hidden,
    context,
    query_weight,
    key_projection_rows,
    value_weight,
    query_lower_factor,
    key_down,
    value_down,
    query_up,
    key_up,
    value_up,
    output_weight,
    output_down,
    output_up,
    slice_group,
):
    groups = slice_group.shape[0]
    nt, nd = lax.axis_size("tensor"), lax.axis_size("dp")
    per, dpg = groups // nt, nd // groups
    rank, cb = query_up.shape
    place = [lax.axis_index(axis).astype(jnp.int32)[None] for axis in ("tensor", "dp")]
    info = jnp.concatenate((place[0], slice_group, place[1]))

    order = list(range(nt // 2, nt)) + list(range(1, nt // 2)) + [0]

    def exchange(sent):
        return {s: swap(x, "tensor", s) if s else x for s, x in sent.items()}

    keyval = pack_key_value(
        info,
        key_projection_rows,
        value_weight,
        key_down.T,
        value_down.T,
        key_up,
        value_up,
        (output_up, query_lower_factor.T),
        nt,
        per,
    )
    got = exchange({s: keyval[s] for s in order})
    keyval = [got[s] for s in range(nt)]
    rb = query_weight.shape[0]
    output_ups = jnp.stack([x[rb : rb + rank, :cb] for x in keyval])
    query_downs = jnp.stack([x[rb + rank :, :rb] for x in keyval])
    outgoing = split_columns(info, output_weight, hidden, (output_down.T, query_up), nd)
    blocks = lax.all_to_all(outgoing, "dp", split_axis=0, concat_axis=0, tiled=True)

    query = []
    for j in range(per):
        sent = {}
        for s in order:
            late = j == 0 and s == 1
            us = EST["pick_query_last" if late else "pick_query"]
            after = keyval[1:] if late else []
            sent[s] = pick_query(info, query_weight, s, j, groups, per, us, after)
        got = exchange(sent)
        query.append([got[s] for s in range(nt)])

    context_all = lax.all_gather(context, "dp", axis=0, tiled=True)

    cols = blocks.shape[2]
    tile = max(128, cols // 16)
    chunks = ((0, 3), (3, 3), (6, 1), (7, 1))
    if cols // tile == 16:
        chunks = ((0, 6), (6, 6), (12, 3), (15, 1))
    merged_output = None
    sums, done = [], []
    for n, (first, count) in enumerate(chunks):
        last = n == len(chunks) - 1
        sent = {}
        for s in order:
            after = []
            if s and n == 0:
                after = query[0][1:] + (query[-1][1:] if s == 1 else [])
            elif s and last:
                after = picked
            elif s and n >= 2:
                after = done[n - 2]
            sent[s] = pick_output(
                info, blocks, rb, output_ups, s, first, count, tile, per, dpg, after
            )
        picked = [sent[s] for s in order if s]
        got = exchange(sent)
        done.append([got[s] for s in order if s])
        if n == 0:
            query_ups = jnp.stack([got[s][:, rb:, :cb] for s in range(nt)])
            merged_qkv, *partial = place_qkv(
                info, blocks, hidden.shape[0], query, keyval, query_downs, query_ups, per, dpg, nd
            )
            projections = total_over("dp", *partial)
        merged_output, send, keep = place_output(
            info, context_all, [got[s] for s in range(nt)], rb, merged_output, first * tile,
            tile * (count if count < 6 else 2), cols, nt,
            partial[:1] if n == 1 else sums[:-1] + [projections] if last else [],
        )
        sums.append(total_over("tensor", send, keep))
    attention_output = jnp.concatenate(sums, axis=1)
    return (merged_qkv, merged_output, projections, attention_output)


def solution(mesh):
    rows = P(("dp", "tensor"), None)
    ups = P(None, ("dp", "tensor"))
    placed = (
        P("dp", None),
        P("dp", "tensor"),
        rows,
        rows,
        rows,
        rows,
        rows,
        rows,
        ups,
        P(),
        P(),
        rows,
        rows,
        ups,
        P(),
    )
    return jax.shard_map(
        body,
        mesh=mesh,
        in_specs=placed,
        out_specs=(P("dp", "tensor"), P("tensor", "dp"), P("dp", "tensor"), P("tensor", "dp")),
        check_vma=False,
    )
```

```python
import functools

import jax
import jax.numpy as jnp
from jax import lax
from jax.experimental import pallas as pl
from jax.experimental.pallas import tpu as pltpu
from jax.sharding import PartitionSpec as P

adapter_scale_factor = 2.0
f32, bf16 = jnp.float32, jnp.bfloat16
PARAMS = dict(vmem_limit_bytes=56 * 1024 * 1024)


def total_over(axis, send, keep):
    n = lax.axis_size(axis)
    for b in range(n.bit_length() - 1):
        total = (keep.astype(f32) + swap(send, axis, 1 << b).astype(f32)).astype(bf16)
        send, keep = total[1::2], total[0::2]
    return keep[0]


def swap(x, axis, mask):
    n = lax.axis_size(axis)
    return lax.ppermute(x, axis, [(i, i ^ mask) for i in range(n)])


def cost(flops, us):
    return pl.CostEstimate(flops=int(us * 1e9), bytes_accessed=0, transcendentals=0)


EST = dict(
    pack_key_value=1,
    split_columns=1,
    pick_output=1,
    place_qkv=1,
    place_output=200,
    pick_query=1,
    pick_query_last=300,
)
ANY = pl.BlockSpec(memory_space=pl.ANY)
VMEM = pl.BlockSpec(memory_space=pltpu.VMEM)


def merged_t(base, down_t, up):
    update = lax.dot_general(down_t, up, (((0,), (0,)), ((), ())), preferred_element_type=f32)
    return (base.astype(f32) + adapter_scale_factor * update).astype(bf16)


def call(kernel, grid, in_specs, out_specs, out_shape, name, us, scratch=(), alias={}):
    return pl.pallas_call(
        kernel,
        grid_spec=pltpu.PrefetchScalarGridSpec(
            num_scalar_prefetch=1,
            grid=grid,
            in_specs=in_specs,
            out_specs=out_specs,
            scratch_shapes=scratch,
        ),
        out_shape=out_shape,
        input_output_aliases=alias,
        compiler_params=pltpu.CompilerParams(**PARAMS),
        cost_estimate=cost(0, us),
        name=name,
    )


def group_of(s, j, i, per):
    return i[1 + (i[0] ^ s) * per + j]


def pack_key_value(info, key_w, value_w, key_dt, value_dt, key_u, value_u, riders, nt, per):
    rb, width = key_w.shape
    hd = width // (nt * per)
    some, wide = riders[0].shape
    count = len(riders)

    def kernel(info_ref, kw, vw, kd, vd, ku, vu, *refs):
        outs, (mk, mv) = refs[count : count + nt], refs[count + nt :]
        mk[...] = merged_t(kw[...], kd[...], ku[...])
        mv[...] = merged_t(vw[...], vd[...], vu[...])
        for s in range(nt):
            for j in range(per):
                at = pl.ds(pl.multiple_of(group_of(s, j, info_ref, per) * hd, hd), hd)
                outs[s][:rb, (2 * j) * hd : (2 * j + 1) * hd] = mk[:, at]
                outs[s][:rb, (2 * j + 1) * hd : (2 * j + 2) * hd] = mv[:, at]
            for n in range(count):
                outs[s][rb + n * some : rb + (n + 1) * some, :wide] = refs[n][...]

    return call(
        kernel,
        (),
        [VMEM] * (6 + count),
        [VMEM] * nt,
        [jax.ShapeDtypeStruct((rb + count * some, per * 2 * hd), bf16)] * nt,
        "pack_key_value",
        EST["pack_key_value"],
        [pltpu.VMEM((rb, width), bf16)] * 2,
    )(info, key_w, value_w, key_dt, value_dt, key_u, value_u, *riders)


def pick_query(info, query_w, s, j, groups, per, us, after):
    rb, width = query_w.shape
    cols = width // groups
    steps = 4

    def kernel(info_ref, q, *refs):
        refs[-1][...] = q[...]

    return call(
        kernel,
        (steps,),
        [pl.BlockSpec((rb // steps, cols), lambda r, i: (r, group_of(s, j, i, per)))]
        + [ANY] * len(after),
        pl.BlockSpec((rb // steps, cols), lambda r, i: (r, 0)),
        jax.ShapeDtypeStruct((rb, cols), bf16),
        f"pick_query_{s}_{j}",
        us,
    )(info, query_w, *after)


def folds(rank, rb, wide):
    return min(wide // rb, rank // 16)


def split_columns(info, weight, tokens, factors, nd):
    rb, width = weight.shape
    more = tokens.shape[0]
    rank = factors[0].shape[0]
    wide = width // nd
    parts = folds(rank, rb, wide)
    few = rank // parts
    rows = rb + more + len(factors) * few

    def kernel(info_ref, w, t, *refs):
        out = refs[-1]
        out[0, :rb, :] = w[...]
        out[0, rb : rb + more, :] = t[...]
        for n in range(len(factors)):
            at = rb + more + n * few
            for p in range(parts):
                out[0, at : at + few, p * rb : (p + 1) * rb] = refs[n][p * few : (p + 1) * few, :]

    return call(
        kernel,
        (nd,),
        [
            pl.BlockSpec((rb, wide), lambda d, i: (0, d)),
            pl.BlockSpec((more, wide), lambda d, i: (0, d)),
        ]
        + [pl.BlockSpec((rank, rb), lambda d, i: (0, 0))] * len(factors),
        pl.BlockSpec((1, rows, wide), lambda d, i: (d, 0, 0)),
        jax.ShapeDtypeStruct((nd, rows, wide), bf16),
        "split_columns",
        EST["split_columns"],
    )(info, weight, tokens, *factors)


def pick_output(info, blocks, rb, ups, s, first, count, tile, per, dpg, after):
    parts = per * dpg
    nt, rank, cb = ups.shape
    width = count * tile
    piece = min(tile, cb)
    pieces = width // piece
    parted = folds(rank, rb, blocks.shape[2])
    few = rank // parted
    end = blocks.shape[1] // few
    more = 0 if first else rank

    def kernel(info_ref, x, *refs):
        d, r = refs[:parted], refs[parted : 2 * parted]
        up, out = refs[2 * parted : 2 * parted + pieces], refs[-1]
        down_t = jnp.concatenate([y[0] for y in d], axis=0)
        out[0, :rb, :] = merged_t(x[0], down_t, jnp.concatenate([u[0] for u in up], axis=1))
        if more:
            for p in range(parted):
                out[0, rb + p * few : rb + (p + 1) * few, :cb] = r[p][0]

    def source(l, i):
        return group_of(s, l // dpg, i, per) * dpg + l % dpg

    def factor_at(row, p, l, i):
        return (source(l, i), row, p)

    def up_at(p, l, i):
        at = first * tile + p * piece
        return ((at // cb) ^ i[0], 0, at % cb // piece)

    return call(
        kernel,
        (parts,),
        [pl.BlockSpec((1, rb, width), lambda l, i: (source(l, i), 0, first // count))]
        + [
            pl.BlockSpec((1, few, cb), functools.partial(factor_at, row, p))
            for row in (end - 2, end - 1)
            for p in range(parted)
        ]
        + [pl.BlockSpec((1, rank, piece), functools.partial(up_at, p)) for p in range(pieces)]
        + [ANY] * len(after),
        pl.BlockSpec((1, rb + more, width), lambda l, i: (l, 0, 0)),
        jax.ShapeDtypeStruct((parts, rb + more, width), bf16),
        f"pick_output_{s}_{first}",
        EST["pick_output"],
    )(info, blocks, *[blocks] * (2 * parted), *[ups] * pieces, *after)


def place_qkv(info, blocks, hidden_rows, query, keyval, downs, ups, per, dpg, nd):
    nt, rank, cb = downs.shape
    rb, gq = query[0][0].shape
    sources, _, depth = blocks.shape
    some = hidden_rows
    count = sources * some
    tile = keyval[0].shape[1] // per
    wide = gq // tile
    each = wide + 1
    cols = per * each * tile
    piece = min(tile, cb)
    pieces = tile // piece

    def kernel(info_ref, a, d, *refs):
        u, refs = refs[:pieces], refs[pieces:]
        full, send, keep, term = refs[-4:]
        place = pl.program_id(0) // each
        last = lax.rem(pl.program_id(0), each) == wide

        def put(blocks):
            total = jnp.zeros((count, tile), f32)
            for s in range(nt):
                at = pl.ds(pl.multiple_of((info_ref[0] ^ s) * rb, rb), rb)
                full[at, :] = blocks[s]
                rows = a[:, :, at].reshape(count, rb)
                total += jnp.dot(rows, blocks[s], preferred_element_type=f32)
            term[...] = total.astype(bf16)
            for s in range(nd):
                at = pl.ds(pl.multiple_of((info_ref[info_ref.shape[0] - 1] ^ s) * some, some), some)
                (send if s % 2 else keep)[s // 2] = term[at, :]

        for j in range(per):
            q = refs[j * nt : (j + 1) * nt]

            @pl.when(jnp.logical_and(place == j, jnp.logical_not(last)))
            def _():
                up = jnp.concatenate([x[0, 0] for x in u], axis=1)
                put([merged_t(q[s][...], d[s], up) for s in range(nt)])

        @pl.when(last)
        def _():
            put([x[...] for x in refs[per * nt : (per + 1) * nt]])

    def column(j, n, i):
        k, w = n // each, jnp.minimum(n % each, wide - 1)
        return (0, jnp.where(k == j, w, jnp.where(k < j, 0, wide - 1)))

    def up_at(p, n, i):
        at = jnp.minimum(n % each, wide - 1) * tile
        block = at // cb + p
        return ((block % nt) ^ i[0], (n // each) * dpg + block // nt, 0, at % cb // piece)

    half = jax.ShapeDtypeStruct((nd // 2, count // nd, cols), bf16)
    half_spec = pl.BlockSpec((nd // 2, count // nd, tile), lambda n, i: (0, 0, n))
    return call(
        kernel,
        (per * each,),
        [
            pl.BlockSpec((sources, some, depth), lambda n, i: (0, rb // some, 0)),
            pl.BlockSpec(downs.shape, lambda n, i: (0, 0, 0)),
        ]
        + [pl.BlockSpec((1, 1, rank, piece), functools.partial(up_at, p)) for p in range(pieces)]
        + [
            pl.BlockSpec((rb, tile), functools.partial(column, j))
            for j in range(per)
            for _ in range(nt)
        ]
        + [pl.BlockSpec((rb, tile), lambda n, i: (0, n // each))] * nt,
        [
            pl.BlockSpec((nt * rb, tile), lambda n, i: (0, n)),
            half_spec,
            half_spec,
        ],
        [jax.ShapeDtypeStruct((nt * rb, cols), bf16), half, half],
        "place_qkv",
        EST["place_qkv"],
        [pltpu.VMEM((count, tile), bf16)],
    )(info, blocks, downs, *[ups] * pieces, *[x for at in query for x in at], *keyval)


def place_output(info, tokens, arrived, rb, before, first, tile, cols, nt, after):
    parts, _, width = arrived[0].shape
    rows, depth = tokens.shape
    each = rows // nt

    def kernel(info_ref, a, *refs):
        full, send, keep, term = refs[-4:]
        total = jnp.zeros((rows, tile), f32)
        for s in range(nt):
            for l in range(parts):
                at = pl.ds(pl.multiple_of((l * nt + (info_ref[0] ^ s)) * rb, rb), rb)
                x = refs[s][l]
                full[at, :] = x
                total += jnp.dot(a[:, at], x, preferred_element_type=f32)
        term[...] = total.astype(bf16)
        for s in range(nt):
            at = pl.ds(pl.multiple_of((info_ref[0] ^ s) * each, each), each)
            (send if s % 2 else keep)[s // 2] = term[at, :]

    operands = [info, tokens, *arrived]
    alias = {}
    if before is not None:
        alias = {len(operands): 0}
        after = [before, *after]
    half = jax.ShapeDtypeStruct((nt // 2, each, width), bf16)
    half_spec = pl.BlockSpec((nt // 2, each, tile), lambda c, i: (0, 0, c))
    return call(
        kernel,
        (width // tile,),
        [pl.BlockSpec((rows, depth), lambda c, i: (0, 0))]
        + [pl.BlockSpec((parts, rb, tile), lambda c, i: (0, 0, c))] * nt
        + [ANY] * len(after),
        [
            pl.BlockSpec((depth, tile), lambda c, i: (0, first // tile + c)),
            half_spec,
            half_spec,
        ],
        [jax.ShapeDtypeStruct((depth, cols), bf16), half, half],
        f"place_output_{first}",
        EST["place_output"],
        [pltpu.VMEM((rows, tile), bf16)],
        alias,
    )(*operands, *after)


def body(
    hidden,
    context,
    query_weight,
    key_projection_rows,
    value_weight,
    query_lower_factor,
    key_down,
    value_down,
    query_up,
    key_up,
    value_up,
    output_weight,
    output_down,
    output_up,
    slice_group,
):
    groups = slice_group.shape[0]
    nt, nd = lax.axis_size("tensor"), lax.axis_size("dp")
    per, dpg = groups // nt, nd // groups
    rank, cb = query_up.shape
    place = [lax.axis_index(axis).astype(jnp.int32)[None] for axis in ("tensor", "dp")]
    info = jnp.concatenate((place[0], slice_group, place[1]))

    order = list(range(nt // 2, nt)) + list(range(1, nt // 2)) + [0]

    def exchange(sent):
        return {s: swap(x, "tensor", s) if s else x for s, x in sent.items()}

    keyval = pack_key_value(
        info,
        key_projection_rows,
        value_weight,
        key_down.T,
        value_down.T,
        key_up,
        value_up,
        (output_up, query_lower_factor.T),
        nt,
        per,
    )
    got = exchange({s: keyval[s] for s in order})
    keyval = [got[s] for s in range(nt)]
    rb = query_weight.shape[0]
    output_ups = jnp.stack([x[rb : rb + rank, :cb] for x in keyval])
    query_downs = jnp.stack([x[rb + rank :, :rb] for x in keyval])
    outgoing = split_columns(info, output_weight, hidden, (output_down.T, query_up), nd)
    blocks = lax.all_to_all(outgoing, "dp", split_axis=0, concat_axis=0, tiled=True)

    query = []
    for j in range(per):
        sent = {}
        for s in order:
            late = j == 0 and s == 1
            us = EST["pick_query_last" if late else "pick_query"]
            after = keyval[1:] if late else []
            sent[s] = pick_query(info, query_weight, s, j, groups, per, us, after)
        got = exchange(sent)
        query.append([got[s] for s in range(nt)])

    context_all = lax.all_gather(context, "dp", axis=0, tiled=True)

    cols = blocks.shape[2]
    tile = max(128, cols // 16)
    chunks = ((0, 3), (3, 3), (6, 1), (7, 1))
    if cols // tile == 16:
        chunks = ((0, 6), (6, 6), (12, 3), (15, 1))
    merged_output = None
    sums, done = [], []
    picks, arrived = [], []
    for n, (first, count) in enumerate(chunks):
        last = n == len(chunks) - 1
        sent = {}
        for s in order:
            after = []
            if s and n == 0:
                after = query[0][1:] + (query[-1][1:] if s == 1 else [])
            elif s and last:
                after = picked
            elif s and n >= 2:
                after = done[n - 2]
            sent[s] = pick_output(
                info, blocks, rb, output_ups, s, first, count, tile, per, dpg, after
            )
        picked = [sent[s] for s in order if s]
        picks.append(picked)
        got = exchange(sent)
        arrived.append(got)
        done.append([got[s] for s in order if s])
    for n, (first, count) in enumerate(chunks):
        last, got = n == len(chunks) - 1, arrived[n]
        if n == 0:
            query_ups = jnp.stack([got[s][:, rb:, :cb] for s in range(nt)])
            merged_qkv, *partial = place_qkv(
                info, blocks, hidden.shape[0], query, keyval, query_downs, query_ups, per, dpg, nd
            )
            projections = total_over("dp", *partial)
        merged_output, send, keep = place_output(
            info, context_all, [got[s] for s in range(nt)], rb, merged_output, first * tile,
            tile * (count if count < 6 else 2), cols, nt,
            partial[:1] + picks[2] if n == 1 else sums[:-1] + [projections] if last else [],
        )
        sums.append(total_over("tensor", send, keep))
    attention_output = jnp.concatenate(sums, axis=1)
    return (merged_qkv, merged_output, projections, attention_output)


def solution(mesh):
    rows = P(("dp", "tensor"), None)
    ups = P(None, ("dp", "tensor"))
    placed = (
        P("dp", None),
        P("dp", "tensor"),
        rows,
        rows,
        rows,
        rows,
        rows,
        rows,
        ups,
        P(),
        P(),
        rows,
        rows,
        ups,
        P(),
    )
    return jax.shard_map(
        body,
        mesh=mesh,
        in_specs=placed,
        out_specs=(P("dp", "tensor"), P("tensor", "dp"), P("dp", "tensor"), P("tensor", "dp")),
        check_vma=False,
    )
```
